32 devices in a mesh: dp: 4 (over y, x), seq: 8 (over z, core).
Axes of the slice: x: 2, y: 2, z: 4, core: 2. Of those that a mesh axis runs over, the one named last changes fastest.
Arguments:
- queries: bfloat16 [4, 3072, 4096], P('dp', 'seq'), may hold values from -0.59765625 to 0.59765625
- keys: bfloat16 [4, 3072, 4096], P('dp', 'seq'), may hold values from -0.59765625 to 0.59765625
- values: bfloat16 [4, 3072, 4096], P('dp', 'seq'), may hold values from -6 to 6
- grad_out: bfloat16 [4, 3072, 4096], P('dp', 'seq'), may hold values from -6 to 6
- gain: float32 [4096], replicated, may hold values from 0.1 to 1.9
Outputs:
- output: bfloat16 [4, 3072, 4096], P('dp', 'seq')
- grad_queries: bfloat16 [4, 3072, 4096], P('dp', 'seq')
- grad_keys: bfloat16 [4, 3072, 4096], P('dp', 'seq')
- grad_values: bfloat16 [4, 3072, 4096], P('dp', 'seq')
- grad_gain: float32 [4096], replicated
The draws below stay inside these ranges and needn't reach their ends.
All inputs are finite; a program needn't handle non-finite values.
Results may differ from the reference program's by a relative error of at most 0.0051.
Values sent between devices are 32-bit elements; how exact they have to be, the bound alone decides.
A program may use at most 192 MiB of HBM per device.

```python
import jax
import jax.numpy as jnp
from jax import lax

H = 32
HD = 128
TOK_DEV = 384
INNER = 4096
TOKENS = 3072
SEQS = 4


def block_scale(rng, shape, shards, least, high):
    loudness, own = 1.0, jax.random.fold_in(rng, 6)
    for axis_at, parts in shards:
        steps = jnp.exp(jax.random.uniform(jax.random.fold_in(own, axis_at), (parts,), jnp.float32, least / len(shards), high / len(shards)))
        loudness = loudness * jnp.repeat(steps, shape[axis_at] // parts).reshape([-1 if axis == axis_at else 1 for axis in range(len(shape))])
    return loudness


def gaussian(key, dims, scale, bound, shards=(), dtype=jnp.bfloat16):
    factor_of = block_scale(key, dims, shards, -0.22, 0.18) if shards else 1.0
    result = jax.random.normal(key, dims, jnp.float32) * scale * factor_of
    return jnp.minimum(jnp.maximum(result, -bound), bound).astype(dtype)


def setup_inputs(seed: int = 0) -> dict:
    splits = jax.random.split(jax.random.key(seed), 6)
    return {
        "queries": gaussian(splits[0], (SEQS, TOKENS, INNER), 0.1, 0.59765625, ((0, 4), (1, 8))),
        "keys": gaussian(splits[1], (SEQS, TOKENS, INNER), 0.1, 0.59765625, ((0, 4), (1, 8))),
        "values": gaussian(splits[2], (SEQS, TOKENS, INNER), 1.0, 6.0, ((0, 4), (1, 8))),
        "grad_out": gaussian(splits[3], (SEQS, TOKENS, INNER), 1.0, 6.0, ((0, 4), (1, 8))),
        "gain": jnp.clip(1.0 + 0.18 * jax.random.normal(splits[4], (INNER,), jnp.float32), 0.1, 1.9),
    }


def causal_mask(count):
    row = lax.broadcasted_iota(jnp.int32, (count, count), 0)
    col = lax.broadcasted_iota(jnp.int32, (count, count), 1)
    return row >= col

def forward_block(items, gain):
    query, key_b, value, grad_b, prefix = items
    count = query.shape[0]
    mask = causal_mask(count)
    qf = query.astype(jnp.float32)
    kf = key_b.astype(jnp.float32)
    vf = value.astype(jnp.float32)
    scores = jnp.einsum('thd,ihd->hti', qf, kf)
    probs = jnp.where(mask[None], scores, 0.0).astype(jnp.bfloat16)
    attn = jnp.einsum('hti,ihe->the', probs.astype(jnp.float32), vf)
    attn = attn + jnp.einsum('thd,hde->the', qf, prefix, precision=lax.Precision.HIGHEST)
    flat = attn.reshape(count, -1)
    rms = jnp.sqrt(lax.optimization_barrier(jnp.mean(flat * flat, axis=-1, keepdims=True)) + 1e-05)
    normed = flat / rms
    output = (normed * gain).astype(jnp.bfloat16)
    upstream = grad_b.astype(jnp.float32)
    gain_term = lax.optimization_barrier(jnp.sum(upstream * normed, axis=0))
    g_normed = upstream * gain
    d_flat = ((g_normed - normed * lax.optimization_barrier(jnp.mean(g_normed * normed, axis=-1, keepdims=True))) / rms).astype(jnp.bfloat16)
    d_attn = d_flat.reshape(query.shape)
    block_grad = jnp.einsum('thd,the->hde', qf, d_attn.astype(jnp.float32))
    return (output, d_attn, gain_term, block_grad)

def backward_block(items):
    query, key_b, value, d_attn, prefix, suffix = items
    count = query.shape[0]
    mask = causal_mask(count)
    qf = query.astype(jnp.float32)
    kf = key_b.astype(jnp.float32)
    vf = value.astype(jnp.float32)
    df = d_attn.astype(jnp.float32)
    scores = jnp.einsum('thd,ihd->hti', qf, kf)
    probs = jnp.where(mask[None], scores, 0.0).astype(jnp.bfloat16).astype(jnp.float32)
    dscores = jnp.einsum('the,ihe->hti', df, vf)
    dprobs = jnp.where(mask[None], dscores, 0.0).astype(jnp.bfloat16).astype(jnp.float32)
    high = lax.Precision.HIGHEST
    grad_q = jnp.einsum('hti,ihd->thd', dprobs, kf) + jnp.einsum('the,hde->thd', df, prefix, precision=high)
    grad_k = jnp.einsum('hti,thd->ihd', dprobs, qf) + jnp.einsum('ihe,hde->ihd', vf, suffix, precision=high)
    grad_v = jnp.einsum('hti,the->ihe', probs, df) + jnp.einsum('ihd,hde->ihe', kf, suffix, precision=high)
    return (grad_q.astype(jnp.bfloat16), grad_k.astype(jnp.bfloat16), grad_v.astype(jnp.bfloat16))

def reference(queries, keys, values, grad_out, gain):
    blocks = TOKENS // TOK_DEV
    outs, gq_all, gk_all, gv_all = ([], [], [], [])
    grad_gain = jnp.zeros((H * HD,), jnp.float32)
    for seq_index in range(SEQS):
        shaped = [a[seq_index].reshape(blocks, TOK_DEV, H, HD) for a in (queries, keys, values, grad_out)]
        query, key_b, value, grad_b = shaped
        states = jnp.einsum('cthd,cthe->chde', key_b.astype(jnp.float32), value.astype(jnp.float32))
        zero = jnp.zeros((1, H, HD, HD), jnp.float32)
        prefix = jnp.concatenate([zero, jnp.cumsum(states, axis=0)[:-1]], axis=0)
        flat_grad = grad_out[seq_index].reshape(blocks, TOK_DEV, H * HD)
        output, d_attn, gain_term, block_grad = lax.map(lambda items: forward_block(items, gain), (query, key_b, value, flat_grad, prefix))
        grad_gain = grad_gain + lax.optimization_barrier(jnp.sum(gain_term, axis=0))
        reverse_sum = jnp.cumsum(block_grad[::-1], axis=0)[::-1]
        suffix = jnp.concatenate([reverse_sum[1:], zero], axis=0)
        grad_q, grad_k, grad_v = lax.map(backward_block, (query, key_b, value, d_attn, prefix, suffix))
        outs.append(output.reshape(TOKENS, H * HD))
        gq_all.append(grad_q.reshape(TOKENS, H * HD))
        gk_all.append(grad_k.reshape(TOKENS, H * HD))
        gv_all.append(grad_v.reshape(TOKENS, H * HD))
    return (jnp.stack(outs), jnp.stack(gq_all), jnp.stack(gk_all), jnp.stack(gv_all), grad_gain)
```

```python
import functools

import jax
import jax.numpy as jnp
from jax import lax
from jax.experimental import pallas as pl
from jax.experimental.pallas import tpu as pltpu
from jax.sharding import PartitionSpec as P

HD = 128
F32 = jnp.float32
BF16 = jnp.bfloat16


def dot(a, b, ca, cb):
    return lax.dot_general(a, b, (((ca,), (cb,)), ((), ())), preferred_element_type=F32)


def split(x):
    hi = x.astype(BF16)
    return hi, (x - hi.astype(F32)).astype(BF16)


def twice(x):
    return jnp.concatenate([x, x], axis=1)


def times_state(x, state):
    hi, lo = split(state)
    return dot(twice(x), jnp.concatenate([hi, lo], axis=0), 1, 0)


def times_state_t(x, state):
    hi, lo = split(state)
    return dot(twice(x), jnp.concatenate([hi, lo], axis=1), 1, 1)


def kernel(
    S, D, T, H,
    q_hbm, k_hbm, v_hbm, g_hbm, gain,
    out_hbm, gq_hbm, gk_hbm, gv_hbm, gg,
    q, k, v, g, acc1, acc2, ob, gqb, gkb, gvb,
    st, base1, psd1, pst1, car1, pcar1, base2, psd2, pst2, car2, pcar2, pre,
    ssq, gdot, gt, gp, dpb, sqb,
    in_sem, out_sem, gk_sem, gv_sem, sems1, sems2, pair_sem, dp_sem, sq_sem,
):
    C = S // 2
    half = H // 2
    inner = H * HD
    s = lax.axis_index("seq")
    d = lax.axis_index("dp")
    c = lax.div(s, 2)
    core = lax.rem(s, 2)
    partner = s + 1 - 2 * core

    def cols(h):
        return pl.ds(pl.multiple_of(h * HD, HD), HD)

    def mine(i):
        return core * half + i

    def other(i):
        return (1 - core) * half + i

    def remote(src, dst, send, recv, axis, peer):
        return pltpu.make_async_remote_copy(
            src_ref=src, dst_ref=dst, send_sem=send, recv_sem=recv,
            device_id={axis: peer}, device_id_type=pl.DeviceIdType.MESH,
        )

    loads = [
        pltpu.make_async_copy(src.at[0], dst, in_sem.at[n])
        for n, (src, dst) in enumerate(((k_hbm, k), (v_hbm, v), (q_hbm, q), (g_hbm, g)))
    ]
    for load in loads:
        load.start()

    barrier = pltpu.get_barrier_semaphore()
    greet = [("seq", partner)]
    greet += [("seq", lax.rem(s + 2 * j, S)) for j in range(1, C)]
    greet += [("dp", lax.rem(d + j, D)) for j in range(1, D)]
    for axis, peer in greet:
        pl.semaphore_signal(
            barrier, inc=1, device_id={axis: peer}, device_id_type=pl.DeviceIdType.MESH
        )
    ssq[...] = jnp.zeros_like(ssq)
    gdot[...] = jnp.zeros_like(gdot)

    @pl.when(c == 0)
    def _():
        car1[...] = jnp.zeros_like(car1)

    @pl.when(c == C - 1)
    def _():
        car2[...] = jnp.zeros_like(car2)

    row = lax.broadcasted_iota(jnp.int32, (T, T), 0)
    col = lax.broadcasted_iota(jnp.int32, (T, T), 1)

    class Scan:
        def __init__(self, forward, base, psd, pst, car, pcar, sems):
            self.base, self.psd, self.pst, self.car, self.pcar = base, psd, pst, car, pcar
            self.sems = sems
            step = 2 if forward else -2
            self.next = lax.rem(s + step + S, S)
            self.first = (c == 0) if forward else (c == C - 1)
            self.last = (c == C - 1) if forward else (c == 0)
            self.lead = (core == 0) if forward else (core == 1)

        def state_copy(self, i):
            return remote(st.at[other(i)], self.pst.at[i], self.sems.at[0, i], self.sems.at[1, i], "seq", partner)

        def carry_copy(self, i):
            return remote(self.base.at[i], self.car.at[i], self.sems.at[2, i], self.sems.at[3, i], "seq", self.next)

        def share_copy(self, i):
            return remote(self.psd.at[i], self.pcar.at[i], self.sems.at[4, i], self.sems.at[5, i], "seq", partner)

        def begin(self, i):
            self.state_copy(i).wait_recv()
            self.base[i] = st[mine(i)] + self.pst[i]

            @pl.when(self.first)
            def _():
                self.carry_copy(i).start()

        def step(self, i):
            @pl.when(jnp.logical_not(self.first))
            def _():
                self.carry_copy(i).wait_recv()

            @pl.when(jnp.logical_not(jnp.logical_or(self.first, self.last)))
            def _():
                self.base[i] = self.base[i] + self.car[i]
                self.carry_copy(i).start()

            came = self.car[i]

            @pl.when(self.lead)
            def _():
                self.psd[i] = came + st[mine(i)]

            @pl.when(jnp.logical_not(self.lead))
            def _():
                self.psd[i] = came

            self.share_copy(i).start()
            return jnp.where(self.lead, came, came + self.pst[i])

        def shared(self, i):
            self.share_copy(i).wait_recv()
            return self.pcar[i]

        def drain_states(self):
            @pl.loop(0, half)
            def _(i):
                self.state_copy(i).wait_send()

        def drain(self):
            @pl.loop(0, half)
            def _(i):
                self.share_copy(i).wait_send()

            @pl.when(jnp.logical_not(self.last))
            def _():
                @pl.loop(0, half)
                def _(i):
                    self.carry_copy(i).wait_send()

    up = Scan(True, base1, psd1, pst1, car1, pcar1, sems1)
    down = Scan(False, base2, psd2, pst2, car2, pcar2, sems2)

    loads[0].wait()
    loads[1].wait()
    pl.semaphore_wait(barrier, len(greet))

    @pl.loop(0, half)
    def _(i):
        for h in (other(i), mine(i)):
            st[h] = dot(k[:, cols(h)], v[:, cols(h)], 0, 0)
        up.state_copy(i).start()

        @pl.when(i >= 1)
        def _():
            up.begin(i - 1)

    up.begin(half - 1)
    loads[2].wait()
    loads[3].wait()

    def inter(h, prefix):
        pre[h] = prefix
        a = acc1[:, cols(h)] + times_state(q[:, cols(h)], prefix)
        acc1[:, cols(h)] = a
        ssq[...] += a * a
        gdot[...] += g[:, cols(h)].astype(F32) * gain[pl.ds(h, 1), :] * a

    @pl.loop(0, half)
    def _(i):
        for h in (mine(i), other(i)):
            scores = dot(q[:, cols(h)], k[:, cols(h)], 1, 1)
            probs = jnp.where(row >= col, scores, 0.0).astype(BF16)
            acc1[:, cols(h)] = dot(probs, v[:, cols(h)], 1, 0)
        inter(mine(i), up.step(i))

        @pl.when(i >= 1)
        def _():
            inter(other(i - 1), up.shared(i - 1))

    inter(other(half - 1), up.shared(half - 1))
    up.drain_states()

    inv = lax.rsqrt(jnp.sum(ssq[...], axis=1, keepdims=True) * (1.0 / inner) + 1e-05)
    mean = jnp.sum(gdot[...], axis=1, keepdims=True) * inv * (1.0 / inner)
    ssq[...] = jnp.broadcast_to(inv, (T, HD))
    gdot[...] = jnp.broadcast_to(mean, (T, HD))

    @pl.loop(0, half)
    def _(i):
        for h in (other(i), mine(i)):
            scale = gain[pl.ds(h, 1), :]
            normed = acc1[:, cols(h)] * ssq[...]
            ob[:, cols(h)] = (normed * scale).astype(BF16)
            upstream = g[:, cols(h)].astype(F32)
            gt[pl.ds(h, 1), :] = jnp.sum(upstream * normed, axis=0, keepdims=True)
            d_attn = ((upstream * scale - normed * gdot[...]) * ssq[...]).astype(BF16)
            g[:, cols(h)] = d_attn
            st[h] = dot(q[:, cols(h)], d_attn, 0, 0)
        down.state_copy(i).start()

        @pl.when(i >= 1)
        def _():
            down.begin(i - 1)

    down.begin(half - 1)
    pair = remote(gt, gp, pair_sem.at[0], pair_sem.at[1], "seq", partner)
    pair.start()
    write_out = pltpu.make_async_copy(ob, out_hbm.at[0], out_sem.at[0])
    write_out.start()
    write_gq = pltpu.make_async_copy(gqb, gq_hbm.at[0], out_sem.at[1])

    def dp_copy(j):
        return remote(dpb.at[d], dpb.at[d], dp_sem.at[0, j], dp_sem.at[1, j], "dp", lax.rem(d + j, D))

    def sq_copy(j):
        return remote(sqb.at[c], sqb.at[c], sq_sem.at[0, j], sq_sem.at[1, j], "seq", lax.rem(s + 2 * j, S))

    def out_copies(h):
        return (
            pltpu.make_async_copy(gkb.at[:, cols(h)], gk_hbm.at[0, :, cols(h)], gk_sem.at[h]),
            pltpu.make_async_copy(gvb.at[:, cols(h)], gv_hbm.at[0, :, cols(h)], gv_sem.at[h]),
        )

    def finish(h, suffix):
        gkb[:, cols(h)] = (acc1[:, cols(h)] + times_state_t(v[:, cols(h)], suffix)).astype(BF16)
        gvb[:, cols(h)] = (acc2[:, cols(h)] + times_state(k[:, cols(h)], suffix)).astype(BF16)
        for copy in out_copies(h):
            copy.start()

    @pl.loop(0, half)
    def _(i):
        for h in (mine(i), other(i)):
            qh, kh, vh, dh = (x[:, cols(h)] for x in (q, k, v, g))
            probs_t = jnp.where(row <= col, dot(kh, qh, 1, 1), 0.0).astype(BF16)
            acc2[:, cols(h)] = dot(probs_t, dh, 1, 0)
            d_probs_t = jnp.where(row <= col, dot(vh, dh, 1, 1), 0.0).astype(BF16)
            acc1[:, cols(h)] = dot(d_probs_t, qh, 1, 0)
            d_probs = jnp.where(row >= col, dot(dh, vh, 1, 1), 0.0).astype(BF16)
            grad_q = dot(d_probs, kh, 1, 0) + times_state_t(dh, pre[h])
            gqb[:, cols(h)] = grad_q.astype(BF16)

        finish(mine(i), down.step(i))

        @pl.when(i >= 1)
        def _():
            finish(other(i - 1), down.shared(i - 1))

        @pl.when(i == half // 4)
        def _():
            pair.wait()
            dpb[d] = gt[...] + gp[...]
            for j in range(1, D):
                dp_copy(j).start()

        @pl.when(i == half // 2)
        def _():
            for j in range(1, D):
                dp_copy(j).wait()
            total = dpb[0]
            for j in range(1, D):
                total = total + dpb[j]
            sqb[c] = total
            for j in range(1, C):
                sq_copy(j).start()

    write_gq.start()
    finish(other(half - 1), down.shared(half - 1))
    for j in range(1, C):
        sq_copy(j).wait()
    total = sqb[0]
    for j in range(1, C):
        total = total + sqb[j]
    gg[...] = total
    up.drain()
    down.drain_states()
    down.drain()
    write_out.wait()
    write_gq.wait()

    @pl.loop(0, H)
    def _(h):
        for copy in out_copies(h):
            copy.wait()


def local(S, D, queries, keys, values, grad_out, gain):
    _, T, inner = queries.shape
    H = inner // HD
    half = H // 2
    big = jax.ShapeDtypeStruct((1, T, inner), BF16)
    anyspec = pl.BlockSpec(memory_space=pl.ANY)
    vmem = pl.BlockSpec(memory_space=pltpu.VMEM)
    wide16 = pltpu.VMEM((T, inner), BF16)
    wide32 = pltpu.VMEM((T, inner), F32)
    part = pltpu.VMEM((half, HD, HD), F32)
    whole = pltpu.VMEM((H, HD, HD), F32)
    row = pltpu.VMEM((H, HD), F32)
    sem = pltpu.SemaphoreType.DMA
    flops = 2 * T * HD * inner * 26
    out = pl.pallas_call(
        functools.partial(kernel, S, D, T, H),
        out_shape=(big, big, big, big, jax.ShapeDtypeStruct((H, HD), F32)),
        in_specs=[anyspec] * 4 + [vmem],
        out_specs=(anyspec,) * 4 + (vmem,),
        scratch_shapes=[wide16] * 4 + [wide32] * 2 + [wide16] * 4
        + [whole] + [part] * 10 + [whole]
        + [pltpu.VMEM((T, HD), F32)] * 2
        + [row, row, pltpu.VMEM((D, H, HD), F32), pltpu.VMEM((S // 2, H, HD), F32)]
        + [sem((4,)), sem((2,)), sem((H,)), sem((H,)), sem((6, half)), sem((6, half)),
           sem((2,)), sem((2, D)), sem((2, S // 2))],
        compiler_params=pltpu.CompilerParams(
            collective_id=0, has_side_effects=True, vmem_limit_bytes=60 * 1024 * 1024
        ),
        cost_estimate=pl.CostEstimate(
            flops=flops, bytes_accessed=8 * T * inner * 2, transcendentals=0
        ),
    )(queries, keys, values, grad_out, gain.reshape(H, HD))
    return out[:4] + (out[4].reshape(inner),)


def solution(mesh):
    wide = P("dp", "seq", None)
    return jax.shard_map(
        functools.partial(local, mesh.shape["seq"], mesh.shape["dp"]),
        mesh=mesh,
        in_specs=(wide, wide, wide, wide, P()),
        out_specs=(wide, wide, wide, wide, P()),
        check_vma=False,
    )
```

```python
import functools

import jax
import jax.numpy as jnp
from jax import lax
from jax.experimental import pallas as pl
from jax.experimental.pallas import tpu as pltpu
from jax.sharding import PartitionSpec as P

HD = 128
F32 = jnp.float32
BF16 = jnp.bfloat16


def dot(a, b, ca, cb):
    return lax.dot_general(a, b, (((ca,), (cb,)), ((), ())), preferred_element_type=F32)


def split(x):
    hi = x.astype(BF16)
    return hi, (x - hi.astype(F32)).astype(BF16)


def twice(x):
    return jnp.concatenate([x, x], axis=1)


def times_state(x, state):
    hi, lo = split(state)
    return dot(twice(x), jnp.concatenate([hi, lo], axis=0), 1, 0)


def times_state_t(x, state):
    hi, lo = split(state)
    return dot(twice(x), jnp.concatenate([hi, lo], axis=1), 1, 1)


def kernel(
    S, D, T, H,
    q_hbm, k_hbm, v_hbm, g_hbm, gain,
    ob, gqb, gkb, gvb, gg,
    q, k, v, g, acc1, acc2,
    st, base1, psd1, pst1, car1, pcar1, base2, psd2, pst2, car2, pcar2, pre,
    ssq, gdot, gt, gp, dpb, sqb,
    in_sem, sems1, sems2, pair_sem, dp_sem, sq_sem,
):
    C = S // 2
    half = H // 2
    inner = H * HD
    s = lax.axis_index("seq")
    d = lax.axis_index("dp")
    c = lax.div(s, 2)
    core = lax.rem(s, 2)
    partner = s + 1 - 2 * core

    def cols(h):
        return pl.ds(pl.multiple_of(h * HD, HD), HD)

    def mine(i):
        return core * half + i

    def other(i):
        return (1 - core) * half + i

    def remote(src, dst, send, recv, axis, peer):
        return pltpu.make_async_remote_copy(
            src_ref=src, dst_ref=dst, send_sem=send, recv_sem=recv,
            device_id={axis: peer}, device_id_type=pl.DeviceIdType.MESH,
        )

    loads = [
        pltpu.make_async_copy(src.at[0], dst, in_sem.at[n])
        for n, (src, dst) in enumerate(((k_hbm, k), (v_hbm, v), (q_hbm, q), (g_hbm, g)))
    ]
    for load in loads:
        load.start()

    barrier = pltpu.get_barrier_semaphore()
    greet = [("seq", partner)]
    greet += [("seq", lax.rem(s + 2 * j, S)) for j in range(1, C)]
    greet += [("dp", lax.rem(d + j, D)) for j in range(1, D)]
    for axis, peer in greet:
        pl.semaphore_signal(
            barrier, inc=1, device_id={axis: peer}, device_id_type=pl.DeviceIdType.MESH
        )
    ssq[...] = jnp.zeros_like(ssq)
    gdot[...] = jnp.zeros_like(gdot)

    @pl.when(c == 0)
    def _():
        car1[...] = jnp.zeros_like(car1)

    @pl.when(c == C - 1)
    def _():
        car2[...] = jnp.zeros_like(car2)

    cut = 2 * HD if T > 2 * HD else T
    later = [(0, cut)] + ([(cut, T)] if cut < T else [])
    early = ([(0, T - cut)] if cut < T else []) + [(T - cut, T)]

    def masked(x, at):
        row = lax.broadcasted_iota(jnp.int32, x.shape, 0) + at
        col = lax.broadcasted_iota(jnp.int32, x.shape, 1)
        return jnp.where(row >= col, x, 0.0).astype(BF16)

    def masked_t(x):
        row = lax.broadcasted_iota(jnp.int32, x.shape, 0)
        col = lax.broadcasted_iota(jnp.int32, x.shape, 1)
        return jnp.where(row <= col, x, 0.0).astype(BF16)

    class Scan:
        def __init__(self, forward, base, psd, pst, car, pcar, sems):
            self.base, self.psd, self.pst, self.car, self.pcar = base, psd, pst, car, pcar
            self.sems = sems
            step = 2 if forward else -2
            self.next = lax.rem(s + step + S, S)
            self.first = (c == 0) if forward else (c == C - 1)
            self.last = (c == C - 1) if forward else (c == 0)
            self.lead = (core == 0) if forward else (core == 1)

        def state_copy(self, i):
            return remote(st.at[other(i)], self.pst.at[i], self.sems.at[0, i], self.sems.at[1, i], "seq", partner)

        def carry_copy(self, i):
            return remote(self.base.at[i], self.car.at[i], self.sems.at[2, i], self.sems.at[3, i], "seq", self.next)

        def share_copy(self, i):
            return remote(self.psd.at[i], self.pcar.at[i], self.sems.at[4, i], self.sems.at[5, i], "seq", partner)

        def begin(self, i):
            self.state_copy(i).wait_recv()
            self.base[i] = st[mine(i)] + self.pst[i]

            @pl.when(self.first)
            def _():
                self.carry_copy(i).start()

        def step(self, i):
            @pl.when(jnp.logical_not(self.first))
            def _():
                self.carry_copy(i).wait_recv()

            @pl.when(jnp.logical_not(jnp.logical_or(self.first, self.last)))
            def _():
                self.base[i] = self.base[i] + self.car[i]
                self.carry_copy(i).start()

            came = self.car[i]

            @pl.when(self.lead)
            def _():
                self.psd[i] = came + st[mine(i)]

            @pl.when(jnp.logical_not(self.lead))
            def _():
                self.psd[i] = came

            self.share_copy(i).start()
            return jnp.where(self.lead, came, came + self.pst[i])

        def shared(self, i):
            self.share_copy(i).wait_recv()
            return self.pcar[i]

        def drain_states(self):
            @pl.loop(0, half)
            def _(i):
                self.state_copy(i).wait_send()

        def drain(self):
            @pl.loop(0, half)
            def _(i):
                self.share_copy(i).wait_send()

            @pl.when(jnp.logical_not(self.last))
            def _():
                @pl.loop(0, half)
                def _(i):
                    self.carry_copy(i).wait_send()

    up = Scan(True, base1, psd1, pst1, car1, pcar1, sems1)
    down = Scan(False, base2, psd2, pst2, car2, pcar2, sems2)

    loads[0].wait()
    loads[1].wait()
    pl.semaphore_wait(barrier, len(greet))

    @pl.loop(0, half)
    def _(i):
        for h in (other(i), mine(i)):
            st[h] = dot(k[:, cols(h)], v[:, cols(h)], 0, 0)
        up.state_copy(i).start()

        @pl.when(i >= 1)
        def _():
            up.begin(i - 1)

    up.begin(half - 1)
    loads[2].wait()
    loads[3].wait()

    def inter(h, prefix):
        pre[h] = prefix
        a = acc1[:, cols(h)] + times_state(q[:, cols(h)], prefix)
        acc1[:, cols(h)] = a
        ssq[...] += a * a
        gdot[...] += g[:, cols(h)].astype(F32) * gain[pl.ds(h, 1), :] * a

    @pl.loop(0, half)
    def _(i):
        for h in (mine(i), other(i)):
            for lo, hi in later:
                probs = masked(dot(q[lo:hi, cols(h)], k[:hi, cols(h)], 1, 1), lo)
                acc1[lo:hi, cols(h)] = dot(probs, v[:hi, cols(h)], 1, 0)
        inter(mine(i), up.step(i))

        @pl.when(i >= 1)
        def _():
            inter(other(i - 1), up.shared(i - 1))

    inter(other(half - 1), up.shared(half - 1))
    up.drain_states()

    inv = lax.rsqrt(jnp.sum(ssq[...], axis=1, keepdims=True) * (1.0 / inner) + 1e-05)
    mean = jnp.sum(gdot[...], axis=1, keepdims=True) * inv * (1.0 / inner)
    ssq[...] = jnp.broadcast_to(inv, (T, HD))
    gdot[...] = jnp.broadcast_to(mean, (T, HD))

    @pl.loop(0, half)
    def _(i):
        for h in (other(i), mine(i)):
            scale = gain[pl.ds(h, 1), :]
            normed = acc1[:, cols(h)] * ssq[...]
            ob[:, cols(h)] = (normed * scale).astype(BF16)
            upstream = g[:, cols(h)].astype(F32)
            gt[pl.ds(h, 1), :] = jnp.sum(upstream * normed, axis=0, keepdims=True)
            d_attn = ((upstream * scale - normed * gdot[...]) * ssq[...]).astype(BF16)
            g[:, cols(h)] = d_attn
            st[h] = dot(q[:, cols(h)], d_attn, 0, 0)
        down.state_copy(i).start()

        @pl.when(i >= 1)
        def _():
            down.begin(i - 1)

    down.begin(half - 1)
    pair = remote(gt, gp, pair_sem.at[0], pair_sem.at[1], "seq", partner)
    pair.start()

    def dp_copy(j):
        return remote(dpb.at[d], dpb.at[d], dp_sem.at[0, j], dp_sem.at[1, j], "dp", lax.rem(d + j, D))

    def sq_copy(j):
        return remote(sqb.at[c], sqb.at[c], sq_sem.at[0, j], sq_sem.at[1, j], "seq", lax.rem(s + 2 * j, S))

    def finish(h, suffix):
        gkb[:, cols(h)] = (acc1[:, cols(h)] + times_state_t(v[:, cols(h)], suffix)).astype(BF16)
        gvb[:, cols(h)] = (acc2[:, cols(h)] + times_state(k[:, cols(h)], suffix)).astype(BF16)

    @pl.loop(0, half)
    def _(i):
        for h in (mine(i), other(i)):
            at = cols(h)
            for lo, hi in early:
                probs_t = masked_t(dot(k[lo:hi, at], q[lo:, at], 1, 1))
                acc2[lo:hi, at] = dot(probs_t, g[lo:, at], 1, 0)
                d_probs_t = masked_t(dot(v[lo:hi, at], g[lo:, at], 1, 1))
                acc1[lo:hi, at] = dot(d_probs_t, q[lo:, at], 1, 0)
            for lo, hi in later:
                d_probs = masked(dot(g[lo:hi, at], v[:hi, at], 1, 1), lo)
                grad_q = dot(d_probs, k[:hi, at], 1, 0) + times_state_t(g[lo:hi, at], pre[h])
                gqb[lo:hi, at] = grad_q.astype(BF16)

        finish(mine(i), down.step(i))

        @pl.when(i >= 1)
        def _():
            finish(other(i - 1), down.shared(i - 1))

        @pl.when(i == half // 4)
        def _():
            pair.wait()
            dpb[d] = gt[...] + gp[...]
            for j in range(1, D):
                dp_copy(j).start()

        @pl.when(i == half // 2)
        def _():
            for j in range(1, D):
                dp_copy(j).wait()
            total = dpb[0]
            for j in range(1, D):
                total = total + dpb[j]
            sqb[c] = total
            for j in range(1, C):
                sq_copy(j).start()

    finish(other(half - 1), down.shared(half - 1))
    for j in range(1, C):
        sq_copy(j).wait()
    total = sqb[0]
    for j in range(1, C):
        total = total + sqb[j]
    gg[...] = total
    up.drain()
    down.drain_states()
    down.drain()


def write(*refs):
    done = refs[10]
    pairs = [(refs[n], refs[5 + n].at[0]) for n in range(4)] + [(refs[4], refs[9])]
    copies = [pltpu.make_async_copy(src, dst, done.at[n]) for n, (src, dst) in enumerate(pairs)]
    for copy in copies:
        copy.start()
    for copy in copies:
        copy.wait()


def local(S, D, queries, keys, values, grad_out, gain):
    _, T, inner = queries.shape
    H = inner // HD
    half = H // 2
    held = pltpu.VMEM((T, inner), BF16)
    big = jax.ShapeDtypeStruct((1, T, inner), BF16)
    anyspec = pl.BlockSpec(memory_space=pl.ANY)
    vmem = pl.BlockSpec(memory_space=pltpu.VMEM)
    wide16 = pltpu.VMEM((T, inner), BF16)
    wide32 = pltpu.VMEM((T, inner), F32)
    part = pltpu.VMEM((half, HD, HD), F32)
    whole = pltpu.VMEM((H, HD, HD), F32)
    row = pltpu.VMEM((H, HD), F32)
    sem = pltpu.SemaphoreType.DMA
    flops = 2 * T * HD * inner * 26
    out = pl.pallas_call(
        functools.partial(kernel, S, D, T, H),
        out_shape=(held, held, held, held, pltpu.VMEM((H, HD), F32)),
        in_specs=[anyspec] * 4 + [vmem],
        out_specs=(vmem,) * 5,
        scratch_shapes=[wide16] * 4 + [wide32] * 2
        + [whole] + [part] * 10 + [whole]
        + [pltpu.VMEM((T, HD), F32)] * 2
        + [row, row, pltpu.VMEM((D, H, HD), F32), pltpu.VMEM((S // 2, H, HD), F32)]
        + [sem((4,)), sem((6, half)), sem((6, half)),
           sem((2,)), sem((2, D)), sem((2, S // 2))],
        compiler_params=pltpu.CompilerParams(
            collective_id=0, has_side_effects=True, vmem_limit_bytes=46 * 1024 * 1024
        ),
        cost_estimate=pl.CostEstimate(
            flops=flops, bytes_accessed=8 * T * inner * 2, transcendentals=0
        ),
    )(queries, keys, values, grad_out, gain.reshape(H, HD))
    wide = pl.pallas_call(
        write,
        out_shape=(big,) * 4 + (jax.ShapeDtypeStruct((H, HD), F32),),
        in_specs=[anyspec] * 5,
        out_specs=(anyspec,) * 5,
        scratch_shapes=[sem((5,))],
        cost_estimate=pl.CostEstimate(flops=0, bytes_accessed=8 * T * inner, transcendentals=0),
    )(*out)
    return tuple(wide[:4]) + (wide[4].reshape(inner),)


def solution(mesh):
    wide = P("dp", "seq", None)
    return jax.shard_map(
        functools.partial(local, mesh.shape["seq"], mesh.shape["dp"]),
        mesh=mesh,
        in_specs=(wide, wide, wide, wide, P()),
        out_specs=(wide, wide, wide, wide, P()),
        check_vma=False,
    )
```

```python
import functools

import jax
import jax.numpy as jnp
from jax import lax
from jax.experimental import pallas as pl
from jax.experimental.pallas import tpu as pltpu
from jax.sharding import PartitionSpec as P

HD = 128
F32 = jnp.float32
BF16 = jnp.bfloat16


def dot(a, b, ca, cb):
    return lax.dot_general(a, b, (((ca,), (cb,)), ((), ())), preferred_element_type=F32)


def split(x):
    hi = x.astype(BF16)
    return hi, (x - hi.astype(F32)).astype(BF16)


def twice(x):
    return jnp.concatenate([x, x], axis=1)


def times_state(x, state):
    hi, lo = split(state)
    return dot(twice(x), jnp.concatenate([hi, lo], axis=0), 1, 0)


def times_state_t(x, state):
    hi, lo = split(state)
    return dot(twice(x), jnp.concatenate([hi, lo], axis=1), 1, 1)


def kernel(
    S, D, T, H,
    q_hbm, k_hbm, v_hbm, g_hbm, gain,
    ob, gqb, gkb, gvb, gg,
    q, k, v, g, acc1, acc2,
    st, base, psd, pst1, car1, pcar1, pst2, car2, pcar2, pre, q_t, probs_a, probs_b,
    ssq, gdot, gt, gp, dpb, sqb,
    in_sem, sems1, sems2, pair_sem, dp_sem, sq_sem,
):
    C = S // 2
    half = H // 2
    inner = H * HD
    s = lax.axis_index("seq")
    d = lax.axis_index("dp")
    c = lax.div(s, 2)
    core = lax.rem(s, 2)
    partner = s + 1 - 2 * core

    def cols(h):
        return pl.ds(pl.multiple_of(h * HD, HD), HD)

    def mine(i):
        return core * half + i

    def other(i):
        return (1 - core) * half + i

    def remote(src, dst, send, recv, axis, peer):
        return pltpu.make_async_remote_copy(
            src_ref=src, dst_ref=dst, send_sem=send, recv_sem=recv,
            device_id={axis: peer}, device_id_type=pl.DeviceIdType.MESH,
        )

    loads = [
        pltpu.make_async_copy(src.at[0], dst, in_sem.at[n])
        for n, (src, dst) in enumerate(((k_hbm, k), (v_hbm, v), (q_hbm, q), (g_hbm, g)))
    ]
    for load in loads:
        load.start()

    barrier = pltpu.get_barrier_semaphore()
    greet = [("seq", partner)]
    greet += [("seq", lax.rem(s + 2 * j, S)) for j in range(1, C)]
    greet += [("dp", lax.rem(d + j, D)) for j in range(1, D)]
    for axis, peer in greet:
        pl.semaphore_signal(
            barrier, inc=1, device_id={axis: peer}, device_id_type=pl.DeviceIdType.MESH
        )
    ssq[...] = jnp.zeros_like(ssq)
    gdot[...] = jnp.zeros_like(gdot)

    @pl.when(c == 0)
    def _():
        car1[...] = jnp.zeros_like(car1)

    @pl.when(c == C - 1)
    def _():
        car2[...] = jnp.zeros_like(car2)

    cut = probs_b.shape[1]
    later = [(0, cut), (cut, T)]
    early = [(0, T - cut), (T - cut, T)]

    def masked(x, at):
        row = lax.broadcasted_iota(jnp.int32, x.shape, 0) + at
        col = lax.broadcasted_iota(jnp.int32, x.shape, 1)
        return jnp.where(row >= col, x, 0.0).astype(BF16)

    def masked_t(x):
        row = lax.broadcasted_iota(jnp.int32, x.shape, 0)
        col = lax.broadcasted_iota(jnp.int32, x.shape, 1)
        return jnp.where(row <= col, x, 0.0).astype(BF16)

    class Scan:
        def __init__(self, forward, base, psd, pst, car, pcar, sems):
            self.base, self.psd, self.pst, self.car, self.pcar = base, psd, pst, car, pcar
            self.sems = sems
            step = 2 if forward else -2
            self.next = lax.rem(s + step + S, S)
            self.first = (c == 0) if forward else (c == C - 1)
            self.last = (c == C - 1) if forward else (c == 0)
            self.lead = (core == 0) if forward else (core == 1)

        def state_copy(self, i):
            return remote(st.at[other(i)], self.pst.at[i], self.sems.at[0, i], self.sems.at[1, i], "seq", partner)

        def carry_copy(self, i):
            return remote(self.base.at[i], self.car.at[i], self.sems.at[2, i], self.sems.at[3, i], "seq", self.next)

        def share_copy(self, i):
            return remote(self.psd.at[i], self.pcar.at[i], self.sems.at[4, i], self.sems.at[5, i], "seq", partner)

        def begin(self, i):
            self.state_copy(i).wait_recv()
            self.base[i] = st[mine(i)] + self.pst[i]

            @pl.when(self.first)
            def _():
                self.carry_copy(i).start()

        def step(self, i):
            @pl.when(jnp.logical_not(self.first))
            def _():
                self.carry_copy(i).wait_recv()

            @pl.when(jnp.logical_not(jnp.logical_or(self.first, self.last)))
            def _():
                self.base[i] = self.base[i] + self.car[i]
                self.carry_copy(i).start()

            came = self.car[i]

            @pl.when(self.lead)
            def _():
                self.psd[i] = came + st[mine(i)]

            @pl.when(jnp.logical_not(self.lead))
            def _():
                self.psd[i] = came

            self.share_copy(i).start()
            return jnp.where(self.lead, came, came + self.pst[i])

        def shared(self, i):
            self.share_copy(i).wait_recv()
            return self.pcar[i]

        def drain_states(self):
            @pl.loop(0, half)
            def _(i):
                self.state_copy(i).wait_send()

        def drain(self):
            @pl.loop(0, half)
            def _(i):
                self.share_copy(i).wait_send()

            @pl.when(jnp.logical_not(self.last))
            def _():
                @pl.loop(0, half)
                def _(i):
                    self.carry_copy(i).wait_send()

    up = Scan(True, base, psd, pst1, car1, pcar1, sems1)
    down = Scan(False, base, psd, pst2, car2, pcar2, sems2)

    loads[0].wait()
    loads[1].wait()
    pl.semaphore_wait(barrier, len(greet))

    @pl.loop(0, half)
    def _(i):
        for h in (other(i), mine(i)):
            st[h] = dot(k[:, cols(h)], v[:, cols(h)], 0, 0)
        up.state_copy(i).start()

        @pl.when(i >= 1)
        def _():
            up.begin(i - 1)

    up.begin(half - 1)
    loads[2].wait()
    loads[3].wait()

    def inter(h, prefix):
        pre[h] = prefix
        a = acc1[:, cols(h)] + times_state(q[:, cols(h)], prefix)
        acc1[:, cols(h)] = a
        ssq[...] += a * a
        gdot[...] += g[:, cols(h)].astype(F32) * gain[pl.ds(h, 1), :] * a

    @pl.loop(0, half)
    def _(i):
        for h in (mine(i), other(i)):
            for lo, hi in later:
                probs = masked(dot(q[lo:hi, cols(h)], k[:hi, cols(h)], 1, 1), lo)
                acc1[lo:hi, cols(h)] = dot(probs, v[:hi, cols(h)], 1, 0)
            for held, (lo, hi) in zip((probs_a, probs_b), early):
                held[h] = masked_t(dot(k[lo:hi, cols(h)], q[lo:, cols(h)], 1, 1))
            q_t[h] = q[:, cols(h)].T
        inter(mine(i), up.step(i))

        @pl.when(i >= 1)
        def _():
            inter(other(i - 1), up.shared(i - 1))

    inter(other(half - 1), up.shared(half - 1))
    up.drain_states()
    up.drain()

    inv = lax.rsqrt(jnp.sum(ssq[...], axis=1, keepdims=True) * (1.0 / inner) + 1e-05)
    mean = jnp.sum(gdot[...], axis=1, keepdims=True) * inv * (1.0 / inner)
    ssq[...] = jnp.broadcast_to(inv, (T, HD))
    gdot[...] = jnp.broadcast_to(mean, (T, HD))

    @pl.loop(0, half)
    def _(i):
        for h in (other(i), mine(i)):
            scale = gain[pl.ds(h, 1), :]
            normed = acc1[:, cols(h)] * ssq[...]
            ob[:, cols(h)] = (normed * scale).astype(BF16)
            upstream = g[:, cols(h)].astype(F32)
            gt[pl.ds(h, 1), :] = jnp.sum(upstream * normed, axis=0, keepdims=True)
            d_attn = ((upstream * scale - normed * gdot[...]) * ssq[...]).astype(BF16)
            g[:, cols(h)] = d_attn
            st[h] = dot(q_t[h], d_attn, 1, 0)
        down.state_copy(i).start()

        @pl.when(i >= 1)
        def _():
            down.begin(i - 1)

    down.begin(half - 1)
    pair = remote(gt, gp, pair_sem.at[0], pair_sem.at[1], "seq", partner)
    pair.start()

    def dp_copy(j):
        return remote(dpb.at[d], dpb.at[d], dp_sem.at[0, j], dp_sem.at[1, j], "dp", lax.rem(d + j, D))

    def sq_copy(j):
        return remote(sqb.at[c], sqb.at[c], sq_sem.at[0, j], sq_sem.at[1, j], "seq", lax.rem(s + 2 * j, S))

    def finish(h, suffix):
        gkb[:, cols(h)] = (acc1[:, cols(h)] + times_state_t(v[:, cols(h)], suffix)).astype(BF16)
        gvb[:, cols(h)] = (acc2[:, cols(h)] + times_state(k[:, cols(h)], suffix)).astype(BF16)

    @pl.loop(0, half)
    def _(i):
        for h in (mine(i), other(i)):
            at = cols(h)
            for held, (lo, hi) in zip((probs_a, probs_b), early):
                acc2[lo:hi, at] = dot(held[h], g[lo:, at], 1, 0)
                d_probs_t = masked_t(dot(v[lo:hi, at], g[lo:, at], 1, 1))
                acc1[lo:hi, at] = dot(d_probs_t, q[lo:, at], 1, 0)
            for lo, hi in later:
                d_probs = masked(dot(g[lo:hi, at], v[:hi, at], 1, 1), lo)
                grad_q = dot(d_probs, k[:hi, at], 1, 0) + times_state_t(g[lo:hi, at], pre[h])
                gqb[lo:hi, at] = grad_q.astype(BF16)

        finish(mine(i), down.step(i))

        @pl.when(i >= 1)
        def _():
            finish(other(i - 1), down.shared(i - 1))

        @pl.when(i == half // 4)
        def _():
            pair.wait()
            dpb[d] = gt[...] + gp[...]
            for j in range(1, D):
                dp_copy(j).start()

        @pl.when(i == half // 2)
        def _():
            for j in range(1, D):
                dp_copy(j).wait()
            total = dpb[0]
            for j in range(1, D):
                total = total + dpb[j]
            sqb[c] = total
            for j in range(1, C):
                sq_copy(j).start()

    finish(other(half - 1), down.shared(half - 1))
    for j in range(1, C):
        sq_copy(j).wait()
    total = sqb[0]
    for j in range(1, C):
        total = total + sqb[j]
    gg[...] = total
    down.drain_states()
    down.drain()


def write(*refs):
    done = refs[10]
    pairs = [(refs[n], refs[5 + n].at[0]) for n in range(4)] + [(refs[4], refs[9])]
    copies = [pltpu.make_async_copy(src, dst, done.at[n]) for n, (src, dst) in enumerate(pairs)]
    for copy in copies:
        copy.start()
    for copy in copies:
        copy.wait()


def local(S, D, queries, keys, values, grad_out, gain):
    _, T, inner = queries.shape
    H = inner // HD
    half = H // 2
    cut = 2 * HD
    held = pltpu.VMEM((T, inner), BF16)
    big = jax.ShapeDtypeStruct((1, T, inner), BF16)
    anyspec = pl.BlockSpec(memory_space=pl.ANY)
    vmem = pl.BlockSpec(memory_space=pltpu.VMEM)
    wide16 = pltpu.VMEM((T, inner), BF16)
    wide32 = pltpu.VMEM((T, inner), F32)
    part = pltpu.VMEM((half, HD, HD), F32)
    whole = pltpu.VMEM((H, HD, HD), F32)
    row = pltpu.VMEM((H, HD), F32)
    sem = pltpu.SemaphoreType.DMA
    flops = 2 * T * HD * inner * 26
    out = pl.pallas_call(
        functools.partial(kernel, S, D, T, H),
        out_shape=(held, held, held, held, pltpu.VMEM((H, HD), F32)),
        in_specs=[anyspec] * 4 + [vmem],
        out_specs=(vmem,) * 5,
        scratch_shapes=[wide16] * 4 + [wide32] * 2
        + [whole] + [part] * 8 + [whole]
        + [pltpu.VMEM((H, HD, T), BF16), pltpu.VMEM((H, T - cut, T), BF16), pltpu.VMEM((H, cut, cut), BF16)]
        + [pltpu.VMEM((T, HD), F32)] * 2
        + [row, row, pltpu.VMEM((D, H, HD), F32), pltpu.VMEM((S // 2, H, HD), F32)]
        + [sem((4,)), sem((6, half)), sem((6, half)),
           sem((2,)), sem((2, D)), sem((2, S // 2))],
        compiler_params=pltpu.CompilerParams(
            collective_id=0, has_side_effects=True, vmem_limit_bytes=49 * 1024 * 1024
        ),
        cost_estimate=pl.CostEstimate(
            flops=flops, bytes_accessed=8 * T * inner * 2, transcendentals=0
        ),
    )(queries, keys, values, grad_out, gain.reshape(H, HD))
    wide = pl.pallas_call(
        write,
        out_shape=(big,) * 4 + (jax.ShapeDtypeStruct((H, HD), F32),),
        in_specs=[vmem] * 5,
        out_specs=(anyspec,) * 5,
        scratch_shapes=[sem((5,))],
        cost_estimate=pl.CostEstimate(flops=0, bytes_accessed=8 * T * inner, transcendentals=0),
        compiler_params=pltpu.CompilerParams(vmem_limit_bytes=16 * 1024 * 1024),
    )(*out)
    return tuple(wide[:4]) + (wide[4].reshape(inner),)


def solution(mesh):
    wide = P("dp", "seq", None)
    return jax.shard_map(
        functools.partial(local, mesh.shape["seq"], mesh.shape["dp"]),
        mesh=mesh,
        in_specs=(wide, wide, wide, wide, P()),
        out_specs=(wide, wide, wide, wide, P()),
        check_vma=False,
    )
```

```python
import functools

import jax
import jax.numpy as jnp
from jax import lax
from jax.experimental import pallas as pl
from jax.experimental.pallas import tpu as pltpu
from jax.sharding import PartitionSpec as P

HD = 128
F32 = jnp.float32
BF16 = jnp.bfloat16


def dot(a, b, ca, cb):
    return lax.dot_general(a, b, (((ca,), (cb,)), ((), ())), preferred_element_type=F32)


def split(x):
    hi = x.astype(BF16)
    return hi, (x - hi.astype(F32)).astype(BF16)


def twice(x):
    return jnp.concatenate([x, x], axis=1)


def times_state(x, state):
    hi, lo = split(state)
    return dot(twice(x), jnp.concatenate([hi, lo], axis=0), 1, 0)


def times_state_t(x, state):
    hi, lo = split(state)
    return dot(twice(x), jnp.concatenate([hi, lo], axis=1), 1, 1)


def kernel(
    S, D, T, H,
    q_hbm, k_hbm, v_hbm, g_hbm, gain,
    ob, gqb, gkb, gvb, gg,
    q, k, v, g, acc1, acc2,
    st, base, psd, pst1, car1, pcar1, pst2, car2, pcar2, pre, q_t, probs_a, probs_b,
    ssq, gdot, gt, gp, dpb, sqb,
    in_sem, sems1, sems2, pair_sem, dp_sem, sq_sem,
):
    C = S // 2
    half = H // 2
    inner = H * HD
    s = lax.axis_index("seq")
    d = lax.axis_index("dp")
    c = lax.div(s, 2)
    core = lax.rem(s, 2)
    partner = s + 1 - 2 * core

    def cols(h):
        return pl.ds(pl.multiple_of(h * HD, HD), HD)

    def mine(i):
        return core * half + i

    def other(i):
        return (1 - core) * half + i

    def remote(src, dst, send, recv, axis, peer):
        return pltpu.make_async_remote_copy(
            src_ref=src, dst_ref=dst, send_sem=send, recv_sem=recv,
            device_id={axis: peer}, device_id_type=pl.DeviceIdType.MESH,
        )

    loads = [
        pltpu.make_async_copy(src.at[0], dst, in_sem.at[n])
        for n, (src, dst) in enumerate(((k_hbm, k), (v_hbm, v), (q_hbm, q), (g_hbm, g)))
    ]
    for load in loads:
        load.start()

    barrier = pltpu.get_barrier_semaphore()
    greet = [("seq", partner)]
    greet += [("seq", lax.rem(s + 2 * j, S)) for j in range(1, C)]
    greet += [("dp", lax.rem(d + j, D)) for j in range(1, D)]
    for axis, peer in greet:
        pl.semaphore_signal(
            barrier, inc=1, device_id={axis: peer}, device_id_type=pl.DeviceIdType.MESH
        )
    ssq[...] = jnp.zeros_like(ssq)
    gdot[...] = jnp.zeros_like(gdot)

    @pl.when(c == 0)
    def _():
        car1[...] = jnp.zeros_like(car1)

    @pl.when(c == C - 1)
    def _():
        car2[...] = jnp.zeros_like(car2)

    cut = probs_b.shape[1]
    later = [(0, cut), (cut, T)]
    early = [(0, T - cut), (T - cut, T)]

    def masked(x, at):
        row = lax.broadcasted_iota(jnp.int32, x.shape, 0) + at
        col = lax.broadcasted_iota(jnp.int32, x.shape, 1)
        return jnp.where(row >= col, x, 0.0).astype(BF16)

    def masked_t(x):
        row = lax.broadcasted_iota(jnp.int32, x.shape, 0)
        col = lax.broadcasted_iota(jnp.int32, x.shape, 1)
        return jnp.where(row <= col, x, 0.0).astype(BF16)

    class Scan:
        def __init__(self, forward, base, psd, pst, car, pcar, sems):
            self.base, self.psd, self.pst, self.car, self.pcar = base, psd, pst, car, pcar
            self.sems = sems
            step = 2 if forward else -2
            self.next = lax.rem(s + step + S, S)
            self.first = (c == 0) if forward else (c == C - 1)
            self.last = (c == C - 1) if forward else (c == 0)
            self.lead = (core == 0) if forward else (core == 1)

        def state_copy(self, i):
            return remote(st.at[other(i)], self.pst.at[i], self.sems.at[0, i], self.sems.at[1, i], "seq", partner)

        def carry_copy(self, i):
            return remote(self.base.at[i], self.car.at[i], self.sems.at[2, i], self.sems.at[3, i], "seq", self.next)

        def share_copy(self, i):
            return remote(self.psd.at[i], self.pcar.at[i], self.sems.at[4, i], self.sems.at[5, i], "seq", partner)

        def begin(self, i):
            self.state_copy(i).wait_recv()
            self.base[i] = st[mine(i)] + self.pst[i]

            @pl.when(self.first)
            def _():
                self.carry_copy(i).start()

        def step(self, i):
            @pl.when(jnp.logical_not(self.first))
            def _():
                self.carry_copy(i).wait_recv()

            @pl.when(jnp.logical_not(jnp.logical_or(self.first, self.last)))
            def _():
                self.base[i] = self.base[i] + self.car[i]
                self.carry_copy(i).start()

            came = self.car[i]

            @pl.when(self.lead)
            def _():
                self.psd[i] = came + st[mine(i)]

            @pl.when(jnp.logical_not(self.lead))
            def _():
                self.psd[i] = came

            self.share_copy(i).start()
            return jnp.where(self.lead, came, came + self.pst[i])

        def shared(self, i):
            self.share_copy(i).wait_recv()
            return self.pcar[i]

        def drain_states(self):
            @pl.loop(0, half)
            def _(i):
                self.state_copy(i).wait_send()

        def drain(self):
            @pl.loop(0, half)
            def _(i):
                self.share_copy(i).wait_send()

            @pl.when(jnp.logical_not(self.last))
            def _():
                @pl.loop(0, half)
                def _(i):
                    self.carry_copy(i).wait_send()

    up = Scan(True, base, psd, pst1, car1, pcar1, sems1)
    down = Scan(False, base, psd, pst2, car2, pcar2, sems2)

    loads[0].wait()
    loads[1].wait()
    pl.semaphore_wait(barrier, len(greet))

    @pl.loop(0, half)
    def _(i):
        for h in (other(i), mine(i)):
            st[h] = dot(k[:, cols(h)], v[:, cols(h)], 0, 0)
        up.state_copy(i).start()

        @pl.when(i >= 1)
        def _():
            up.begin(i - 1)

    up.begin(half - 1)
    loads[2].wait()
    loads[3].wait()

    def inter(h, prefix):
        pre[h] = prefix
        a = acc1[:, cols(h)] + times_state(q[:, cols(h)], prefix)
        acc1[:, cols(h)] = a
        ssq[...] += a * a
        gdot[...] += g[:, cols(h)].astype(F32) * gain[pl.ds(h, 1), :] * a

    ahead_up = half * c // (2 * C)
    gap = C - 1 - c
    ahead_down = half * gap * gap * gap // (C - 1) ** 3

    def forward_blocks(i):
        for h in (mine(i), other(i)):
            for lo, hi in later:
                probs = masked(dot(q[lo:hi, cols(h)], k[:hi, cols(h)], 1, 1), lo)
                acc1[lo:hi, cols(h)] = dot(probs, v[:hi, cols(h)], 1, 0)
            for held, (lo, hi) in zip((probs_a, probs_b), early):
                held[h] = masked_t(dot(k[lo:hi, cols(h)], q[lo:, cols(h)], 1, 1))
            q_t[h] = q[:, cols(h)].T

    @pl.loop(0, ahead_up)
    def _(i):
        forward_blocks(i)

    @pl.loop(0, half)
    def _(i):
        @pl.when(i + ahead_up < half)
        def _():
            forward_blocks(i + ahead_up)

        inter(mine(i), up.step(i))

        @pl.when(i >= 1)
        def _():
            inter(other(i - 1), up.shared(i - 1))

    inter(other(half - 1), up.shared(half - 1))
    up.drain_states()
    up.drain()

    inv = lax.rsqrt(jnp.sum(ssq[...], axis=1, keepdims=True) * (1.0 / inner) + 1e-05)
    mean = jnp.sum(gdot[...], axis=1, keepdims=True) * inv * (1.0 / inner)
    ssq[...] = jnp.broadcast_to(inv, (T, HD))
    gdot[...] = jnp.broadcast_to(mean, (T, HD))

    @pl.loop(0, half)
    def _(i):
        for h in (other(i), mine(i)):
            scale = gain[pl.ds(h, 1), :]
            normed = acc1[:, cols(h)] * ssq[...]
            ob[:, cols(h)] = (normed * scale).astype(BF16)
            upstream = g[:, cols(h)].astype(F32)
            gt[pl.ds(h, 1), :] = jnp.sum(upstream * normed, axis=0, keepdims=True)
            d_attn = ((upstream * scale - normed * gdot[...]) * ssq[...]).astype(BF16)
            g[:, cols(h)] = d_attn
            st[h] = dot(q_t[h], d_attn, 1, 0)
        down.state_copy(i).start()

        @pl.when(i >= 1)
        def _():
            down.begin(i - 1)

    down.begin(half - 1)
    pair = remote(gt, gp, pair_sem.at[0], pair_sem.at[1], "seq", partner)
    pair.start()

    def dp_copy(j):
        return remote(dpb.at[d], dpb.at[d], dp_sem.at[0, j], dp_sem.at[1, j], "dp", lax.rem(d + j, D))

    def sq_copy(j):
        return remote(sqb.at[c], sqb.at[c], sq_sem.at[0, j], sq_sem.at[1, j], "seq", lax.rem(s + 2 * j, S))

    def finish(h, suffix):
        gkb[:, cols(h)] = (acc1[:, cols(h)] + times_state_t(v[:, cols(h)], suffix)).astype(BF16)
        gvb[:, cols(h)] = (acc2[:, cols(h)] + times_state(k[:, cols(h)], suffix)).astype(BF16)

    def backward_blocks(i):
        for h in (mine(i), other(i)):
            at = cols(h)
            for held, (lo, hi) in zip((probs_a, probs_b), early):
                acc2[lo:hi, at] = dot(held[h], g[lo:, at], 1, 0)
                d_probs_t = masked_t(dot(v[lo:hi, at], g[lo:, at], 1, 1))
                acc1[lo:hi, at] = dot(d_probs_t, q[lo:, at], 1, 0)
            for lo, hi in later:
                d_probs = masked(dot(g[lo:hi, at], v[:hi, at], 1, 1), lo)
                grad_q = dot(d_probs, k[:hi, at], 1, 0) + times_state_t(g[lo:hi, at], pre[h])
                gqb[lo:hi, at] = grad_q.astype(BF16)

    @pl.loop(0, ahead_down)
    def _(i):
        backward_blocks(i)

    @pl.loop(0, half)
    def _(i):
        @pl.when(i + ahead_down < half)
        def _():
            backward_blocks(i + ahead_down)

        finish(mine(i), down.step(i))

        @pl.when(i >= 1)
        def _():
            finish(other(i - 1), down.shared(i - 1))

        @pl.when(i == half // 4)
        def _():
            pair.wait()
            dpb[d] = gt[...] + gp[...]
            for j in range(1, D):
                dp_copy(j).start()

        @pl.when(i == half // 2)
        def _():
            for j in range(1, D):
                dp_copy(j).wait()
            total = dpb[0]
            for j in range(1, D):
                total = total + dpb[j]
            sqb[c] = total
            for j in range(1, C):
                sq_copy(j).start()

    finish(other(half - 1), down.shared(half - 1))
    for j in range(1, C):
        sq_copy(j).wait()
    total = sqb[0]
    for j in range(1, C):
        total = total + sqb[j]
    gg[...] = total
    down.drain_states()
    down.drain()


def write(*refs):
    done = refs[10]
    pairs = [(refs[n], refs[5 + n].at[0]) for n in range(4)] + [(refs[4], refs[9])]
    copies = [pltpu.make_async_copy(src, dst, done.at[n]) for n, (src, dst) in enumerate(pairs)]
    for copy in copies:
        copy.start()
    for copy in copies:
        copy.wait()


def local(S, D, queries, keys, values, grad_out, gain):
    _, T, inner = queries.shape
    H = inner // HD
    half = H // 2
    cut = 2 * HD
    held = pltpu.VMEM((T, inner), BF16)
    big = jax.ShapeDtypeStruct((1, T, inner), BF16)
    anyspec = pl.BlockSpec(memory_space=pl.ANY)
    vmem = pl.BlockSpec(memory_space=pltpu.VMEM)
    wide16 = pltpu.VMEM((T, inner), BF16)
    wide32 = pltpu.VMEM((T, inner), F32)
    part = pltpu.VMEM((half, HD, HD), F32)
    whole = pltpu.VMEM((H, HD, HD), F32)
    row = pltpu.VMEM((H, HD), F32)
    sem = pltpu.SemaphoreType.DMA
    flops = 2 * T * HD * inner * 26
    out = pl.pallas_call(
        functools.partial(kernel, S, D, T, H),
        out_shape=(held, held, held, held, pltpu.VMEM((H, HD), F32)),
        in_specs=[anyspec] * 4 + [vmem],
        out_specs=(vmem,) * 5,
        scratch_shapes=[wide16] * 4 + [wide32] * 2
        + [whole] + [part] * 8 + [whole]
        + [pltpu.VMEM((H, HD, T), BF16), pltpu.VMEM((H, T - cut, T), BF16), pltpu.VMEM((H, cut, cut), BF16)]
        + [pltpu.VMEM((T, HD), F32)] * 2
        + [row, row, pltpu.VMEM((D, H, HD), F32), pltpu.VMEM((S // 2, H, HD), F32)]
        + [sem((4,)), sem((6, half)), sem((6, half)),
           sem((2,)), sem((2, D)), sem((2, S // 2))],
        compiler_params=pltpu.CompilerParams(
            collective_id=0, has_side_effects=True, vmem_limit_bytes=49 * 1024 * 1024
        ),
        cost_estimate=pl.CostEstimate(
            flops=flops, bytes_accessed=8 * T * inner * 2, transcendentals=0
        ),
    )(queries, keys, values, grad_out, gain.reshape(H, HD))
    wide = pl.pallas_call(
        write,
        out_shape=(big,) * 4 + (jax.ShapeDtypeStruct((H, HD), F32),),
        in_specs=[vmem] * 5,
        out_specs=(anyspec,) * 5,
        scratch_shapes=[sem((5,))],
        cost_estimate=pl.CostEstimate(flops=0, bytes_accessed=8 * T * inner, transcendentals=0),
        compiler_params=pltpu.CompilerParams(vmem_limit_bytes=16 * 1024 * 1024),
    )(*out)
    return tuple(wide[:4]) + (wide[4].reshape(inner),)


def solution(mesh):
    wide = P("dp", "seq", None)
    return jax.shard_map(
        functools.partial(local, mesh.shape["seq"], mesh.shape["dp"]),
        mesh=mesh,
        in_specs=(wide, wide, wide, wide, P()),
        out_specs=(wide, wide, wide, wide, P()),
        check_vma=False,
    )
```
